32 devices in a mesh: groups: 2 (over y), col: 4 (over z), row: 2 (over x), sub: 2 (over core).
Axes of the slice: x: 2, y: 2, z: 4, core: 2. Of those that a mesh axis runs over, the one named last changes fastest.
Arguments:
- integrals: bfloat16 [32768, 16384], P(('groups', 'row', 'sub'), 'col'), parts along dimension 0, may hold values from -0.046875 to 0.046875
- integral_mask: int32 [256, 128], P(('groups', 'row', 'sub'), 'col'), parts along dimension 0, may hold values 0 or 1
- amplitudes: bfloat16 [32768, 512], P(('groups', 'col'), ('row', 'sub')), parts along dimension 0, may hold values from -6 to 6
- amplitude_mask: int32 [256, 4], P(('groups', 'col'), ('row', 'sub')), parts along dimension 0, may hold values 0 or 1
- tile_map: int32 [128], replicated, may hold values from 0 to 127, as said below
- row_gap: float32 [32768], P(('groups', 'row', 'sub')), parts along dimension 0, may hold values from 0.3 to 3
- col_gap: float32 [1024], P(('groups', 'col')), parts along dimension 0, may hold values from 0.3 to 3
Outputs:
- cycle_update: bfloat16 [32768, 512], P(('groups', 'row', 'sub'), 'col'), parts along dimension 0
The draws below stay inside these ranges and needn't reach their ends.
There are 2 independent parts, one for each index of `groups`. The reference program is written for one: setup_inputs(seed, part) draws one part's arguments, and reference() takes and returns one part's arrays. A program takes and returns all parts, laid end to end along the dimension named above; an argument that names none is the same for every part. Nothing has to cross between parts.
Inputs may be any that keep to these rules, and one draw needn't show every extreme that they name: tile_map is a permutation of the 128 row tiles. Taking the pair-order row tiles in 4 aligned blocks of 32 and the particle-hole row tiles likewise, every pair block sends exactly max(1, 8) tiles to each particle-hole block that it sends any to, and every particle-hole block receives 128 / 4 tiles.
All inputs are finite; a program needn't handle non-finite values. No bound on the sum of `integral_mask` or of `amplitude_mask` on one device may be relied on, other than what follows from the above.
Results may differ from the reference program's by a relative error of at most 0.012.
Values may be sent and summed in bfloat16 or wider, within the bound.
A program may use at most 128 MiB of HBM per device.

```python
import math
import jax
import jax.numpy as jnp
from jax import lax

TILE = 128
KT = 128
NJT = 4
ORDER = 16384
NCOL = 512
N_COL = 4


def shuffled_rows(key, count, length):
    subkeys = jax.random.split(key, count)

    def one_row(subkey):
        return jax.random.permutation(subkey, length)
    return jax.vmap(one_row)(subkeys)


def draw_tile_map(key, part):
    key = jax.random.fold_in(key, 11)
    held_tiles = KT // N_COL
    owners = N_COL
    subkeys = jax.random.split(key, 4)
    spread = jax.random.permutation(subkeys[0], owners).astype(jnp.int32)
    offset = jax.random.permutation(subkeys[1], owners).astype(jnp.int32)
    within = shuffled_rows(subkeys[2], owners, held_tiles).astype(jnp.int32)
    landing = shuffled_rows(subkeys[3], owners, held_tiles).astype(jnp.int32)
    target = spread[(offset[:, None] + within) % owners]
    slot_index = landing[target, within]
    return (target * held_tiles + slot_index).reshape(KT).astype(jnp.int32)


def place_ends(result, key, low, largest):
    shape = result.shape
    spot = [jax.random.randint(jax.random.fold_in(key, axis), (), 0, shape[axis]) for axis in range(len(shape))]
    result = result.at[tuple(spot)].set(low)
    longest = shape.index(max(shape))
    spot[longest] = (spot[longest] + 1) % shape[longest]
    return result.at[tuple(spot)].set(largest)


def levels(key, dims, cuts, least, high):
    def one(position, blocks):
        heights = jax.random.uniform(jax.random.fold_in(jax.random.fold_in(key, 6), position), (blocks,), jnp.float32, least / len(cuts), high / len(cuts))
        return jnp.repeat(jnp.exp(heights), dims[position] // blocks).reshape((-1,) + (1,) * (len(dims) - position - 1))

    level = one(*cuts[0])
    for cut in cuts[1:]:
        level = level * one(*cut)
    return level


def centred(rng, dims, deviation, limit, cuts=(), held_as=jnp.bfloat16):
    entries = jax.random.normal(rng, dims, jnp.float32) * deviation
    if len(cuts) > 0:
        entries = levels(rng, dims, cuts, -0.22, 0.18) * entries
    return jnp.clip(entries, min=-limit, max=limit).astype(held_as)


def setup_inputs(seed: int = 0, part: int = 0) -> dict:
    key_of = jax.random.split(jax.random.key(seed), 8)
    part_splits = jax.random.split(jax.random.fold_in(key_of[7], part), 8)
    return {
        "integrals": centred(part_splits[0], (ORDER, ORDER), ORDER ** -0.5, 0.046875, ((0, 4), (1, 4))),
        "integral_mask": place_ends((jax.random.randint(part_splits[1], (KT, KT), 0, 4) < 3).astype(jnp.int32), jax.random.fold_in(part_splits[1], 1), 0, 1),
        "amplitudes": centred(part_splits[2], (ORDER, NCOL), 1.0, 6.0, ((0, 4), (1, 4))),
        "amplitude_mask": place_ends((jax.random.randint(part_splits[3], (KT, NJT), 0, 4) < 3).astype(jnp.int32), jax.random.fold_in(part_splits[3], 1), 0, 1),
        "tile_map": draw_tile_map(jax.random.fold_in(key_of[7], 71), part),
        "row_gap": jnp.clip(jnp.exp(math.log(3.0) - 2.3025851 * jax.random.uniform(part_splits[5], (ORDER,), jnp.float32) ** levels(part_splits[5], (ORDER,), ((0, 4),), -0.2, 0.2)), 0.3, 3.0),
        "col_gap": jnp.clip(jnp.exp(math.log(3.0) - 2.3025851 * jax.random.uniform(part_splits[6], (NCOL,), jnp.float32) ** levels(part_splits[6], (NCOL,), ((0, 4),), -0.2, 0.2)), 0.3, 3.0),
    }


def reference(integrals, integral_mask, amplitudes, amplitude_mask, tile_map, row_gap, col_gap):
    block_rows = ORDER // N_COL
    block_tiles = KT // N_COL
    shaped = amplitudes.reshape(KT, TILE, NJT, TILE)
    keeper = (amplitude_mask > 0)[:, None, :, None]
    screened = jnp.where(keeper, shaped, jnp.zeros_like(shaped)).reshape(KT, TILE, NCOL)
    slab_tiles = jnp.zeros_like(screened).at[tile_map].set(screened)
    slab_matrix = slab_tiles.reshape(ORDER, NCOL)

    def add_block(running, index):
        start = (index * block_rows).astype(jnp.int32)
        tile_start = (index * block_tiles).astype(jnp.int32)
        columns = lax.dynamic_slice_in_dim(integrals, start, block_rows, 1)
        screen = lax.dynamic_slice_in_dim(integral_mask, tile_start, block_tiles, 1)
        columns = columns.reshape(KT, TILE, block_tiles, TILE)
        columns = jnp.where((screen > 0)[:, None, :, None], columns, jnp.zeros_like(columns))
        columns = columns.reshape(ORDER, block_rows)
        slab_rows = lax.dynamic_slice_in_dim(slab_matrix, start, block_rows, 0)
        partial_value = jnp.dot(columns, slab_rows, preferred_element_type=jnp.float32).astype(jnp.bfloat16)
        partial_value = lax.optimization_barrier(partial_value)
        return running + partial_value.astype(jnp.float32), None

    initial = jnp.zeros((ORDER, NCOL), jnp.float32)
    contracted, unused = lax.scan(add_block, initial, jnp.arange(N_COL, dtype=jnp.int32))
    scaled = contracted / (row_gap[:, None] + col_gap[None, :])
    return scaled.astype(jnp.bfloat16)
```

```python
import functools

import jax
import jax.numpy as jnp
from jax import lax
from jax.experimental import pallas as pl
from jax.experimental.pallas import tpu as pltpu
from jax.sharding import PartitionSpec as P

TILE = 128
MESH = pl.DeviceIdType.MESH


def largest_block(size, most):
    block = min(size, most)
    while size % block:
        block -= TILE
    return block


def kernel(
    n_col, n_row, n_sub, cap,
    index_ref, mask_ref, amp_ref, row_gap_ref, col_gap_ref, w_ref,
    out_ref,
    w_buf, send_buf, recv_buf, slab, part, sums,
    w_sem, a_send, a_recv, b_send, b_recv, s_send, s_recv,
):
    col = lax.axis_index("col")
    row = lax.axis_index("row")
    sub = lax.axis_index("sub")
    here = row * n_sub + sub
    n_j = n_row * n_sub
    rows, depth = w_buf.shape
    held = depth // TILE
    width = part.shape[2]
    block = largest_block(rows, 256)
    n_block = rows // block
    mm_block = largest_block(rows, 512)
    n_mm = rows // mm_block
    n_w = w_sem.shape[0]
    w_part = rows // n_w

    def w_copy(k):
        view = pl.ds(pl.multiple_of(k * w_part, TILE), w_part)
        return pltpu.make_async_copy(w_ref.at[view], w_buf.at[view], w_sem.at[k])

    for k in range(n_w):
        w_copy(k).start()

    barrier = pltpu.get_barrier_semaphore()
    for k in range(1, n_col):
        pl.semaphore_signal(barrier, inc=1, device_id={"col": (col + k) % n_col}, device_id_type=MESH)
    for k in range(1, n_row):
        pl.semaphore_signal(barrier, inc=1, device_id={"row": (row + k) % n_row}, device_id_type=MESH)
    for k in range(1, n_sub):
        pl.semaphore_signal(barrier, inc=1, device_id={"sub": (sub + k) % n_sub}, device_id_type=MESH)

    @pl.loop(0, n_col * cap)
    def _(q):
        keep = index_ref[n_col * cap + held + q].astype(jnp.float32)
        tile = amp_ref[index_ref[q]].astype(jnp.float32)
        send_buf[q] = (tile * keep).astype(jnp.bfloat16)

    pl.semaphore_wait(barrier, n_col - 1 + n_row - 1 + n_sub - 1)

    def rows_of(s):
        return pl.ds(s * cap, cap)

    def a_copy(k):
        target = (col + k) % n_col
        return pltpu.make_async_remote_copy(
            src_ref=send_buf.at[rows_of(target)],
            dst_ref=recv_buf.at[here, rows_of(col)],
            send_sem=a_send.at[k],
            recv_sem=a_recv.at[k],
            device_id={"col": target},
            device_id_type=MESH,
        )

    def spread(j, s, slot, device):
        return pltpu.make_async_remote_copy(
            src_ref=recv_buf.at[j, rows_of(s)],
            dst_ref=recv_buf.at[j, rows_of(s)],
            send_sem=b_send.at[slot, s],
            recv_sem=b_recv.at[j, s],
            device_id=device,
            device_id_type=MESH,
        )

    for k in range(1, n_col):
        a_copy(k).start()
    recv_buf[here, rows_of(col)] = send_buf[rows_of(col)]

    lane_tile = lax.broadcasted_iota(jnp.int32, (held, depth), 1) // TILE
    tile_row = lax.broadcasted_iota(jnp.int32, (held, depth), 0)
    expand = jnp.where(lane_tile == tile_row, 1.0, 0.0).astype(jnp.bfloat16)
    wide_mask = jnp.dot(
        mask_ref[...].astype(jnp.bfloat16), expand, preferred_element_type=jnp.float32
    ).astype(jnp.bfloat16)

    row_tiles = rows // TILE
    part_tiles = w_part // TILE

    def screen(k):
        w_copy(k).wait()
        for i in range(part_tiles):
            it = k * part_tiles + i
            keep = jnp.broadcast_to(wide_mask[it : it + 1, :], (16, depth))

            @pl.loop(0, TILE // 16)
            def _(r):
                view = pl.ds(pl.multiple_of(it * TILE + r * 16, 16), 16)
                w_buf[view, :] = w_buf[view, :] * keep

    def source(k):
        return (col + n_col - k) % n_col

    def relay(k):
        s = source(k)
        for r in range(1, n_row):
            j = ((row + r) % n_row) * n_sub + sub
            spread(j, s, 0, {"row": row} if n_sub == 1 else {"sub": (sub + 1) % n_sub}).wait_recv()
            for u in range(1, n_sub):
                spread(j, s, n_row - 1 + r * (n_sub - 1) + u - 1, {"sub": (sub + u) % n_sub}).start()

    for k in range(n_col):
        s = source(k)
        if k > 0:
            a_copy(k).wait_recv()
        for r in range(1, n_row):
            spread(here, s, r - 1, {"row": (row + r) % n_row}).start()
        for u in range(1, n_sub):
            spread(here, s, n_row - 1 + u - 1, {"sub": (sub + u) % n_sub}).start()
        if k < n_w:
            screen(k)
        if k > 0:
            relay(k - 1)
    relay(n_col - 1)
    for k in range(n_col):
        s = source(k)
        for u in range(1, n_sub):
            for r in range(n_row):
                j = ((row + r) % n_row) * n_sub + (sub + u) % n_sub
                spread(j, s, 0, {"sub": (sub + 1) % n_sub}).wait_recv()

    @pl.loop(0, held)
    def _(k):
        slot = index_ref[n_col * cap + k]
        for j in range(n_j):
            slab[pl.ds(pl.multiple_of(k * TILE, TILE), TILE), j * TILE : (j + 1) * TILE] = recv_buf[j, slot]

    def s_copy(t, m, right):
        view = pl.ds(pl.multiple_of(m * block, TILE), block)
        return pltpu.make_async_remote_copy(
            src_ref=part.at[t, view],
            dst_ref=sums.at[0 if right else 1, t, view],
            send_sem=s_send.at[t, m],
            recv_sem=s_recv.at[0 if right else 1, t, m],
            device_id={"col": (col + (1 if right else n_col - 1)) % n_col},
            device_id_type=MESH,
        )

    n_cols = n_col * width
    n_wide = largest_block(n_cols, 256)

    @pl.loop(0, n_mm)
    def _(m):
        view = pl.ds(pl.multiple_of(m * mm_block, TILE), mm_block)
        for n in range(n_cols // n_wide):
            product = jnp.dot(
                w_buf[view, :], slab[:, n * n_wide : (n + 1) * n_wide], preferred_element_type=jnp.float32
            ).astype(jnp.bfloat16)
            for t in range(n_wide // width):
                part[n * (n_wide // width) + t, view, :] = product[:, t * width : (t + 1) * width]
        for i in range(mm_block // block):
            at = m * (mm_block // block) + i

            @pl.when(col == 0)
            def _():
                for t in range(n_col - 1, 0, -1):
                    s_copy(t, at, True).start()

            @pl.when(col == n_col - 1)
            def _():
                for t in range(n_col - 1):
                    s_copy(t, at, False).start()

    inner = jnp.logical_and(col > 0, col < n_col - 1)

    @pl.loop(0, n_block)
    def _(m):
        view = pl.ds(pl.multiple_of(m * block, TILE), block)
        for t in range(n_col - 1, 0, -1):

            @pl.when(jnp.logical_and(inner, col < t))
            def _():
                s_copy(t, m, True).wait_recv()
                total = part[t, view, :].astype(jnp.float32) + sums[0, t, view, :].astype(jnp.float32)
                part[t, view, :] = total.astype(jnp.bfloat16)
                s_copy(t, m, True).start()

        for t in range(n_col - 1):

            @pl.when(jnp.logical_and(inner, col > t))
            def _():
                s_copy(t, m, False).wait_recv()
                total = part[t, view, :].astype(jnp.float32) + sums[1, t, view, :].astype(jnp.float32)
                part[t, view, :] = total.astype(jnp.bfloat16)
                s_copy(t, m, False).start()

        def gaps():
            pieces = []
            for i in range(block // TILE):
                line = row_gap_ref[pl.ds(m * (block // TILE) + i, 1), :]
                pieces.append(jnp.broadcast_to(line, (TILE, TILE)).T)
            return jnp.concatenate(pieces, axis=0) + col_gap_ref[...]

        @pl.when(col == 0)
        def _():
            s_copy(0, m, False).wait_recv()
            total = part[0, view, :].astype(jnp.float32) + sums[1, 0, view, :].astype(jnp.float32)
            out_ref[view, :] = (total / gaps()).astype(jnp.bfloat16)

        @pl.when(col == n_col - 1)
        def _():
            s_copy(n_col - 1, m, True).wait_recv()
            total = part[n_col - 1, view, :].astype(jnp.float32) + sums[0, n_col - 1, view, :].astype(jnp.float32)
            out_ref[view, :] = (total / gaps()).astype(jnp.bfloat16)

        @pl.when(inner)
        def _():
            s_copy(col, m, True).wait_recv()
            s_copy(col, m, False).wait_recv()
            total = part[col, view, :].astype(jnp.float32) + sums[0, col, view, :].astype(jnp.float32)
            total = total + sums[1, col, view, :].astype(jnp.float32)
            out_ref[view, :] = (total / gaps()).astype(jnp.bfloat16)

    for k in range(1, n_col):
        a_copy(k).wait_send()
    for k in range(n_col):
        for slot in range(n_row - 1 + n_row * (n_sub - 1)):
            spread(here, k, slot, {"sub": (sub + 1) % n_sub}).wait_send()

    @pl.loop(0, n_block)
    def _(m):
        for t in range(n_col):

            @pl.when(col != t)
            def _():
                s_copy(t, m, True).wait_send()


def per_device(integrals, integral_mask, amplitudes, amplitude_mask, tile_map, row_gap, col_gap, *, n_row, n_sub):
    position = lax.axis_index("col")
    held = amplitudes.shape[0] // TILE
    total = tile_map.shape[0]
    n_col = total // held
    cap = max(1, held // n_col)
    width = col_gap.shape[0]
    rows, depth = integrals.shape
    n_j = n_row * n_sub
    n_block = rows // largest_block(rows, 256)

    every = jnp.arange(total, dtype=jnp.int32)
    owner = tile_map // held
    home = every // held
    earlier = (home[:, None] == home[None, :]) & (owner[:, None] == owner[None, :]) & (every[:, None] < every[None, :])
    rank = jnp.sum(earlier.astype(jnp.int32), axis=0)
    slots = n_col * cap
    line = jnp.arange(2 * slots + held, dtype=jnp.int32)[:, None]
    sent = (home == position)[None, :] & ((owner * cap + rank)[None, :] == line % (slots + held))
    kept = jnp.tile(amplitude_mask.reshape(held), n_col)
    landed = tile_map[None, :] == position * held + line - slots
    index = jnp.sum(
        jnp.where(
            line < slots,
            jnp.where(sent, (every % held)[None, :], 0),
            jnp.where(
                line < slots + held,
                jnp.where(landed, (home * cap + rank)[None, :], 0),
                jnp.where(sent, kept[None, :], 0),
            ),
        ),
        axis=1,
    )

    smem = pl.BlockSpec(memory_space=pltpu.SMEM)
    vmem = pl.BlockSpec(memory_space=pltpu.VMEM)
    dma = pltpu.SemaphoreType.DMA
    return pl.pallas_call(
        functools.partial(kernel, n_col, n_row, n_sub, cap),
        out_shape=jax.ShapeDtypeStruct((rows, width), jnp.bfloat16),
        in_specs=[smem, vmem, vmem, vmem, vmem, pl.BlockSpec(memory_space=pl.ANY)],
        out_specs=vmem,
        scratch_shapes=[
            pltpu.VMEM((rows, depth), jnp.bfloat16),
            pltpu.VMEM((slots, TILE, TILE), jnp.bfloat16),
            pltpu.VMEM((n_j, slots, TILE, TILE), jnp.bfloat16),
            pltpu.VMEM((depth, n_j * TILE), jnp.bfloat16),
            pltpu.VMEM((n_col, rows, width), jnp.bfloat16),
            pltpu.VMEM((2, n_col, rows, width), jnp.bfloat16),
            dma((min(n_col, rows // TILE),)),
            dma((n_col,)),
            dma((n_col,)),
            dma((n_row - 1 + n_row * (n_sub - 1), n_col)),
            dma((n_j, n_col)),
            dma((n_col, n_block)),
            dma((2, n_col, n_block)),
        ],
        compiler_params=pltpu.CompilerParams(
            collective_id=0, has_side_effects=True, vmem_limit_bytes=62 * 1024 * 1024
        ),
        cost_estimate=pl.CostEstimate(
            flops=2 * rows * depth * n_j * TILE, bytes_accessed=2 * rows * depth, transcendentals=0
        ),
    )(
        index,
        integral_mask,
        amplitudes.reshape(held, TILE, TILE),
        row_gap.reshape(rows // TILE, TILE),
        col_gap.reshape(1, width),
        integrals,
    )


def solution(mesh):
    return jax.shard_map(
        functools.partial(per_device, n_row=mesh.shape["row"], n_sub=mesh.shape["sub"]),
        mesh=mesh,
        in_specs=(
            P(("groups", "row", "sub"), "col"),
            P(("groups", "row", "sub"), "col"),
            P(("groups", "col"), ("row", "sub")),
            P(("groups", "col"), ("row", "sub")),
            P(),
            P(("groups", "row", "sub")),
            P(("groups", "col")),
        ),
        out_specs=P(("groups", "row", "sub"), "col"),
        check_vma=False,
    )
```

```python
import functools

import jax
import jax.numpy as jnp
from jax import lax
from jax.experimental import pallas as pl
from jax.experimental.pallas import tpu as pltpu
from jax.sharding import PartitionSpec as P

TILE = 128
MESH = pl.DeviceIdType.MESH


def largest_block(size, most):
    block = min(size, most)
    while size % block:
        block -= TILE
    return block


def kernel(
    n_col, n_row, n_sub, cap,
    index_ref, mask_ref, amp_ref, row_gap_ref, col_gap_ref, w_ref,
    out_ref,
    w_buf, send_buf, recv_buf, slab, part, sums,
    w_sem, a_send, a_recv, b_send, b_recv, s_send, s_recv,
):
    col = lax.axis_index("col")
    row = lax.axis_index("row")
    sub = lax.axis_index("sub")
    here = row * n_sub + sub
    n_j = n_row * n_sub
    rows, depth = w_buf.shape
    held = depth // TILE
    width = part.shape[2]
    block = largest_block(rows, 256)
    n_block = rows // block
    mm_block = largest_block(rows, 512)
    n_w = w_sem.shape[0]
    w_part = rows // n_w

    def w_copy(k):
        view = pl.ds(pl.multiple_of(k * w_part, TILE), w_part)
        return pltpu.make_async_copy(w_ref.at[view], w_buf.at[view], w_sem.at[k])

    for k in range(n_w):
        w_copy(k).start()

    barrier = pltpu.get_barrier_semaphore()
    for k in range(1, n_col):
        pl.semaphore_signal(barrier, inc=1, device_id={"col": (col + k) % n_col}, device_id_type=MESH)
    for k in range(1, n_row):
        pl.semaphore_signal(barrier, inc=1, device_id={"row": (row + k) % n_row}, device_id_type=MESH)
    for k in range(1, n_sub):
        pl.semaphore_signal(barrier, inc=1, device_id={"sub": (sub + k) % n_sub}, device_id_type=MESH)

    @pl.loop(0, n_col * cap)
    def _(q):
        keep = index_ref[n_col * cap + held + q].astype(jnp.float32)
        tile = amp_ref[index_ref[q]].astype(jnp.float32)
        send_buf[q] = (tile * keep).astype(jnp.bfloat16)

    pl.semaphore_wait(barrier, n_col - 1 + n_row - 1 + n_sub - 1)

    def rows_of(s):
        return pl.ds(s * cap, cap)

    nearest = [sorted(range(n_col), key=lambda s: (abs(s - c), abs(2 * s + 1 - n_col))) for c in range(n_col)]

    def source(k):
        found = col * 0
        for c in range(n_col):
            found = jnp.where(col == c, nearest[c][k], found)
        return found

    def a_copy(target, origin):
        return pltpu.make_async_remote_copy(
            src_ref=send_buf.at[rows_of(target)],
            dst_ref=recv_buf.at[here, rows_of(col)],
            send_sem=a_send.at[target],
            recv_sem=a_recv.at[origin],
            device_id={"col": target},
            device_id_type=MESH,
        )

    def spread(j, s, slot, device):
        return pltpu.make_async_remote_copy(
            src_ref=recv_buf.at[j, rows_of(s)],
            dst_ref=recv_buf.at[j, rows_of(s)],
            send_sem=b_send.at[slot, s],
            recv_sem=b_recv.at[j, s],
            device_id=device,
            device_id_type=MESH,
        )

    for k in range(1, n_col):
        a_copy(source(k), col).start()
    recv_buf[here, rows_of(col)] = send_buf[rows_of(col)]

    lane_tile = lax.broadcasted_iota(jnp.int32, (held, depth), 1) // TILE
    tile_row = lax.broadcasted_iota(jnp.int32, (held, depth), 0)
    expand = jnp.where(lane_tile == tile_row, 1.0, 0.0).astype(jnp.bfloat16)
    wide_mask = jnp.dot(
        mask_ref[...].astype(jnp.bfloat16), expand, preferred_element_type=jnp.float32
    ).astype(jnp.bfloat16)

    row_tiles = rows // TILE
    part_tiles = w_part // TILE

    def screen(k):
        w_copy(k).wait()
        for i in range(part_tiles):
            it = k * part_tiles + i
            keep = jnp.broadcast_to(wide_mask[it : it + 1, :], (16, depth))

            @pl.loop(0, TILE // 16)
            def _(r):
                view = pl.ds(pl.multiple_of(it * TILE + r * 16, 16), 16)
                w_buf[view, :] = w_buf[view, :] * keep

    def relay(k):
        s = source(k)
        for r in range(1, n_row):
            j = ((row + r) % n_row) * n_sub + sub
            spread(j, s, 0, {"row": row} if n_sub == 1 else {"sub": (sub + 1) % n_sub}).wait_recv()
            for u in range(1, n_sub):
                spread(j, s, n_row - 1 + r * (n_sub - 1) + u - 1, {"sub": (sub + u) % n_sub}).start()

    for k in range(n_col):
        s = source(k)
        if k > 0:
            a_copy(s, s).wait_recv()
        for r in range(1, n_row):
            spread(here, s, r - 1, {"row": (row + r) % n_row}).start()
        for u in range(1, n_sub):
            spread(here, s, n_row - 1 + u - 1, {"sub": (sub + u) % n_sub}).start()
        if k < n_w:
            screen(k)
        if k > 0:
            relay(k - 1)
    relay(n_col - 1)
    for k in range(n_col):
        s = source(k)
        for u in range(1, n_sub):
            for r in range(n_row):
                j = ((row + r) % n_row) * n_sub + (sub + u) % n_sub
                spread(j, s, 0, {"sub": (sub + 1) % n_sub}).wait_recv()

    @pl.loop(0, held)
    def _(k):
        slot = index_ref[n_col * cap + k]
        for j in range(n_j):
            slab[pl.ds(pl.multiple_of(k * TILE, TILE), TILE), j * TILE : (j + 1) * TILE] = recv_buf[j, slot]

    def s_copy(t, m, right):
        view = pl.ds(pl.multiple_of(m * block, TILE), block)
        return pltpu.make_async_remote_copy(
            src_ref=part.at[t, view],
            dst_ref=sums.at[0 if right else 1, t, view],
            send_sem=s_send.at[t, m],
            recv_sem=s_recv.at[0 if right else 1, t, m],
            device_id={"col": (col + (1 if right else n_col - 1)) % n_col},
            device_id_type=MESH,
        )

    n_cols = n_col * width
    n_wide = largest_block(n_cols, 256)

    inner = jnp.logical_and(col > 0, col < n_col - 1)
    per_mm = mm_block // block

    def gaps(m):
        pieces = []
        for i in range(block // TILE):
            line = row_gap_ref[pl.ds(m * (block // TILE) + i, 1), :]
            pieces.append(jnp.broadcast_to(line, (TILE, TILE)).T)
        return jnp.concatenate(pieces, axis=0) + col_gap_ref[...]

    def relay_sums(m, right):
        view = pl.ds(pl.multiple_of(m * block, TILE), block)
        for t in range(n_col - 1, 0, -1) if right else range(n_col - 1):

            @pl.when(col < t if right else col > t)
            def _():
                s_copy(t, m, right).wait_recv()
                total = part[t, view, :].astype(jnp.float32) + sums[0 if right else 1, t, view, :].astype(jnp.float32)
                part[t, view, :] = total.astype(jnp.bfloat16)
                s_copy(t, m, right).start()

    def finish(m, from_left, from_right):
        view = pl.ds(pl.multiple_of(m * block, TILE), block)
        total = part[col, view, :].astype(jnp.float32)
        if from_left:
            s_copy(col, m, True).wait_recv()
            total = total + sums[0, col, view, :].astype(jnp.float32)
        if from_right:
            s_copy(col, m, False).wait_recv()
            total = total + sums[1, col, view, :].astype(jnp.float32)
        out_ref[view, :] = (total / gaps(m)).astype(jnp.bfloat16)

    lag = 3
    right_lag = lag * (col - 1)
    left_lag = lag * (n_col - 2 - col)
    last_lag = lag * (n_col - 2)

    @pl.loop(0, n_block + last_lag)
    def _(step):
        @pl.when(jnp.logical_and(step < n_block, step % per_mm == 0))
        def _():
            view = pl.ds(pl.multiple_of(step * block, TILE), mm_block)
            for n in range(n_cols // n_wide):
                product = jnp.dot(
                    w_buf[view, :], slab[:, n * n_wide : (n + 1) * n_wide], preferred_element_type=jnp.float32
                ).astype(jnp.bfloat16)
                for t in range(n_wide // width):
                    part[n * (n_wide // width) + t, view, :] = product[:, t * width : (t + 1) * width]

        @pl.when(jnp.logical_and(step < n_block, col == 0))
        def _():
            for t in range(n_col - 1, 0, -1):
                s_copy(t, step, True).start()

        @pl.when(jnp.logical_and(step < n_block, col == n_col - 1))
        def _():
            for t in range(n_col - 1):
                s_copy(t, step, False).start()

        def within(m):
            return jnp.logical_and(inner, jnp.logical_and(m >= 0, m < n_block))

        @pl.when(within(step - right_lag))
        def _():
            relay_sums(step - right_lag, True)

        @pl.when(within(step - left_lag))
        def _():
            relay_sums(step - left_lag, False)

        @pl.when(within(step - last_lag))
        def _():
            finish(step - last_lag, True, True)

    @pl.when(col == 0)
    def _():
        @pl.loop(0, n_block)
        def _(m):
            finish(m, False, True)

    @pl.when(col == n_col - 1)
    def _():
        @pl.loop(0, n_block)
        def _(m):
            finish(m, True, False)

    for k in range(1, n_col):
        a_copy(source(k), col).wait_send()
    for k in range(n_col):
        for slot in range(n_row - 1 + n_row * (n_sub - 1)):
            spread(here, k, slot, {"sub": (sub + 1) % n_sub}).wait_send()

    @pl.loop(0, n_block)
    def _(m):
        for t in range(n_col):

            @pl.when(col != t)
            def _():
                s_copy(t, m, True).wait_send()


def per_device(integrals, integral_mask, amplitudes, amplitude_mask, tile_map, row_gap, col_gap, *, n_row, n_sub):
    position = lax.axis_index("col")
    held = amplitudes.shape[0] // TILE
    total = tile_map.shape[0]
    n_col = total // held
    cap = max(1, held // n_col)
    width = col_gap.shape[0]
    rows, depth = integrals.shape
    n_j = n_row * n_sub
    n_block = rows // largest_block(rows, 256)

    every = jnp.arange(total, dtype=jnp.int32)
    owner = tile_map // held
    home = every // held
    earlier = (home[:, None] == home[None, :]) & (owner[:, None] == owner[None, :]) & (every[:, None] < every[None, :])
    rank = jnp.sum(earlier.astype(jnp.int32), axis=0)
    slots = n_col * cap
    line = jnp.arange(2 * slots + held, dtype=jnp.int32)[:, None]
    sent = (home == position)[None, :] & ((owner * cap + rank)[None, :] == line % (slots + held))
    kept = jnp.tile(amplitude_mask.reshape(held), n_col)
    landed = tile_map[None, :] == position * held + line - slots
    index = jnp.sum(
        jnp.where(
            line < slots,
            jnp.where(sent, (every % held)[None, :], 0),
            jnp.where(
                line < slots + held,
                jnp.where(landed, (home * cap + rank)[None, :], 0),
                jnp.where(sent, kept[None, :], 0),
            ),
        ),
        axis=1,
    )

    smem = pl.BlockSpec(memory_space=pltpu.SMEM)
    vmem = pl.BlockSpec(memory_space=pltpu.VMEM)
    dma = pltpu.SemaphoreType.DMA
    return pl.pallas_call(
        functools.partial(kernel, n_col, n_row, n_sub, cap),
        out_shape=jax.ShapeDtypeStruct((rows, width), jnp.bfloat16),
        in_specs=[smem, vmem, vmem, vmem, vmem, pl.BlockSpec(memory_space=pl.ANY)],
        out_specs=vmem,
        scratch_shapes=[
            pltpu.VMEM((rows, depth), jnp.bfloat16),
            pltpu.VMEM((slots, TILE, TILE), jnp.bfloat16),
            pltpu.VMEM((n_j, slots, TILE, TILE), jnp.bfloat16),
            pltpu.VMEM((depth, n_j * TILE), jnp.bfloat16),
            pltpu.VMEM((n_col, rows, width), jnp.bfloat16),
            pltpu.VMEM((2, n_col, rows, width), jnp.bfloat16),
            dma((min(n_col, rows // TILE),)),
            dma((n_col,)),
            dma((n_col,)),
            dma((n_row - 1 + n_row * (n_sub - 1), n_col)),
            dma((n_j, n_col)),
            dma((n_col, n_block)),
            dma((2, n_col, n_block)),
        ],
        compiler_params=pltpu.CompilerParams(
            collective_id=0, has_side_effects=True, vmem_limit_bytes=62 * 1024 * 1024
        ),
        cost_estimate=pl.CostEstimate(
            flops=2 * rows * depth * n_j * TILE, bytes_accessed=2 * rows * depth, transcendentals=0
        ),
    )(
        index,
        integral_mask,
        amplitudes.reshape(held, TILE, TILE),
        row_gap.reshape(rows // TILE, TILE),
        col_gap.reshape(1, width),
        integrals,
    )


def solution(mesh):
    return jax.shard_map(
        functools.partial(per_device, n_row=mesh.shape["row"], n_sub=mesh.shape["sub"]),
        mesh=mesh,
        in_specs=(
            P(("groups", "row", "sub"), "col"),
            P(("groups", "row", "sub"), "col"),
            P(("groups", "col"), ("row", "sub")),
            P(("groups", "col"), ("row", "sub")),
            P(),
            P(("groups", "row", "sub")),
            P(("groups", "col")),
        ),
        out_specs=P(("groups", "row", "sub"), "col"),
        check_vma=False,
    )
```

```python
import functools

import jax
import jax.numpy as jnp
from jax import lax
from jax.experimental import pallas as pl
from jax.experimental.pallas import tpu as pltpu
from jax.sharding import PartitionSpec as P

TILE = 128
MESH = pl.DeviceIdType.MESH


def largest_block(size, most):
    block = min(size, most)
    while size % block:
        block -= TILE
    return block


def kernel(
    n_col, n_row, n_sub, cap,
    index_ref, mask_ref, amp_ref, row_gap_ref, col_gap_ref, w_ref,
    out_ref,
    w_buf, send_buf, recv_buf, slab, part, sums,
    w_sem, a_send, a_recv, b_send, b_recv, s_send, s_recv,
):
    col = lax.axis_index("col")
    row = lax.axis_index("row")
    sub = lax.axis_index("sub")
    here = row * n_sub + sub
    n_j = n_row * n_sub
    rows, depth = w_buf.shape
    held = depth // TILE
    width = part.shape[2]
    block = largest_block(rows, 256)
    n_block = rows // block
    mm_block = largest_block(rows, 512)
    n_w = w_sem.shape[0]
    w_part = rows // n_w

    def w_copy(k):
        view = pl.ds(pl.multiple_of(k * w_part, TILE), w_part)
        return pltpu.make_async_copy(w_ref.at[view], w_buf.at[view], w_sem.at[k])


    barrier = pltpu.get_barrier_semaphore()
    for k in range(1, n_col):
        pl.semaphore_signal(barrier, inc=1, device_id={"col": (col + k) % n_col}, device_id_type=MESH)
    for k in range(1, n_row):
        pl.semaphore_signal(barrier, inc=1, device_id={"row": (row + k) % n_row}, device_id_type=MESH)
    for k in range(1, n_sub):
        pl.semaphore_signal(barrier, inc=1, device_id={"sub": (sub + k) % n_sub}, device_id_type=MESH)

    @pl.loop(0, n_col * cap)
    def _(q):
        keep = index_ref[n_col * cap + held + q].astype(jnp.float32)
        tile = amp_ref[index_ref[q]].astype(jnp.float32)
        send_buf[q] = (tile * keep).astype(jnp.bfloat16)

    pl.semaphore_wait(barrier, n_col - 1 + n_row - 1 + n_sub - 1)

    def rows_of(s):
        return pl.ds(s * cap, cap)

    nearest = [sorted(range(n_col), key=lambda s: (abs(s - c), abs(2 * s + 1 - n_col))) for c in range(n_col)]

    def source(k):
        found = col * 0
        for c in range(n_col):
            found = jnp.where(col == c, nearest[c][k], found)
        return found

    def a_copy(target, origin):
        return pltpu.make_async_remote_copy(
            src_ref=send_buf.at[rows_of(target)],
            dst_ref=recv_buf.at[here, rows_of(col)],
            send_sem=a_send.at[target],
            recv_sem=a_recv.at[origin],
            device_id={"col": target},
            device_id_type=MESH,
        )

    def spread(j, s, slot, device):
        return pltpu.make_async_remote_copy(
            src_ref=recv_buf.at[j, rows_of(s)],
            dst_ref=recv_buf.at[j, rows_of(s)],
            send_sem=b_send.at[slot, s],
            recv_sem=b_recv.at[j, s],
            device_id=device,
            device_id_type=MESH,
        )

    for k in range(n_col - 1, 0, -1):
        a_copy(source(k), col).start()
    recv_buf[here, rows_of(col)] = send_buf[rows_of(col)]

    lane_tile = lax.broadcasted_iota(jnp.int32, (held, depth), 1) // TILE
    tile_row = lax.broadcasted_iota(jnp.int32, (held, depth), 0)
    expand = jnp.where(lane_tile == tile_row, 1.0, 0.0).astype(jnp.bfloat16)
    wide_mask = jnp.dot(
        mask_ref[...].astype(jnp.bfloat16), expand, preferred_element_type=jnp.float32
    ).astype(jnp.bfloat16)

    row_tiles = rows // TILE
    part_tiles = w_part // TILE

    def screen(k):
        w_copy(k).wait()
        for i in range(part_tiles):
            it = k * part_tiles + i
            keep = jnp.broadcast_to(wide_mask[it : it + 1, :], (16, depth))

            @pl.loop(0, TILE // 16)
            def _(r):
                view = pl.ds(pl.multiple_of(it * TILE + r * 16, 16), 16)
                w_buf[view, :] = w_buf[view, :] * keep

    def relay(k):
        s = source(k)
        for r in range(1, n_row):
            j = ((row + r) % n_row) * n_sub + sub
            spread(j, s, 0, {"row": row} if n_sub == 1 else {"sub": (sub + 1) % n_sub}).wait_recv()
            for u in range(1, n_sub):
                spread(j, s, n_row - 1 + r * (n_sub - 1) + u - 1, {"sub": (sub + u) % n_sub}).start()

    for k in range(n_col):
        s = source(k)
        if k > 0:
            a_copy(s, s).wait_recv()
        for r in range(1, n_row):
            spread(here, s, r - 1, {"row": (row + r) % n_row}).start()
        for u in range(1, n_sub):
            spread(here, s, n_row - 1 + u - 1, {"sub": (sub + u) % n_sub}).start()
        if k == 0:
            for i in range(n_w):
                w_copy(i).start()
        if k < n_w:
            screen(k)
        if k > 0:
            relay(k - 1)
    relay(n_col - 1)
    for k in range(n_col):
        s = source(k)
        for u in range(1, n_sub):
            for r in range(n_row):
                j = ((row + r) % n_row) * n_sub + (sub + u) % n_sub
                spread(j, s, 0, {"sub": (sub + 1) % n_sub}).wait_recv()

    @pl.loop(0, held)
    def _(k):
        slot = index_ref[n_col * cap + k]
        for j in range(n_j):
            slab[pl.ds(pl.multiple_of(k * TILE, TILE), TILE), j * TILE : (j + 1) * TILE] = recv_buf[j, slot]

    def s_copy(t, m, right):
        view = pl.ds(pl.multiple_of(m * block, TILE), block)
        return pltpu.make_async_remote_copy(
            src_ref=part.at[t, view],
            dst_ref=sums.at[0 if right else 1, t, view],
            send_sem=s_send.at[t, m],
            recv_sem=s_recv.at[0 if right else 1, t, m],
            device_id={"col": (col + (1 if right else n_col - 1)) % n_col},
            device_id_type=MESH,
        )

    n_cols = n_col * width
    n_wide = largest_block(n_cols, 256)

    inner = jnp.logical_and(col > 0, col < n_col - 1)
    per_mm = mm_block // block

    def gaps(m):
        pieces = []
        for i in range(block // TILE):
            line = row_gap_ref[pl.ds(m * (block // TILE) + i, 1), :]
            pieces.append(jnp.broadcast_to(line, (TILE, TILE)).T)
        return jnp.concatenate(pieces, axis=0) + col_gap_ref[...]

    def relay_sums(m, right):
        view = pl.ds(pl.multiple_of(m * block, TILE), block)
        for t in range(n_col - 1, 0, -1) if right else range(n_col - 1):

            @pl.when(col < t if right else col > t)
            def _():
                s_copy(t, m, right).wait_recv()
                total = part[t, view, :].astype(jnp.float32) + sums[0 if right else 1, t, view, :].astype(jnp.float32)
                part[t, view, :] = total.astype(jnp.bfloat16)
                s_copy(t, m, right).start()

    def finish(m, from_left, from_right):
        view = pl.ds(pl.multiple_of(m * block, TILE), block)
        total = part[col, view, :].astype(jnp.float32)
        if from_left:
            s_copy(col, m, True).wait_recv()
            total = total + sums[0, col, view, :].astype(jnp.float32)
        if from_right:
            s_copy(col, m, False).wait_recv()
            total = total + sums[1, col, view, :].astype(jnp.float32)
        out_ref[view, :] = (total / gaps(m)).astype(jnp.bfloat16)

    lag = 2
    right_lag = lag * (col - 1)
    left_lag = lag * (n_col - 2 - col)
    last_lag = lag * (n_col - 2)

    @pl.loop(0, n_block + last_lag)
    def _(step):
        @pl.when(jnp.logical_and(step < n_block, step % per_mm == 0))
        def _():
            view = pl.ds(pl.multiple_of(step * block, TILE), mm_block)
            for n in range(n_cols // n_wide):
                product = jnp.dot(
                    w_buf[view, :], slab[:, n * n_wide : (n + 1) * n_wide], preferred_element_type=jnp.float32
                ).astype(jnp.bfloat16)
                for t in range(n_wide // width):
                    part[n * (n_wide // width) + t, view, :] = product[:, t * width : (t + 1) * width]

        @pl.when(jnp.logical_and(step < n_block, col == 0))
        def _():
            for t in range(n_col - 1, 0, -1):
                s_copy(t, step, True).start()

        @pl.when(jnp.logical_and(step < n_block, col == n_col - 1))
        def _():
            for t in range(n_col - 1):
                s_copy(t, step, False).start()

        def within(m):
            return jnp.logical_and(inner, jnp.logical_and(m >= 0, m < n_block))

        @pl.when(within(step - right_lag))
        def _():
            relay_sums(step - right_lag, True)

        @pl.when(within(step - left_lag))
        def _():
            relay_sums(step - left_lag, False)

        @pl.when(within(step - last_lag))
        def _():
            finish(step - last_lag, True, True)

    @pl.when(col == 0)
    def _():
        @pl.loop(0, n_block)
        def _(m):
            finish(m, False, True)

    @pl.when(col == n_col - 1)
    def _():
        @pl.loop(0, n_block)
        def _(m):
            finish(m, True, False)

    for k in range(1, n_col):
        a_copy(source(k), col).wait_send()
    for k in range(n_col):
        for slot in range(n_row - 1 + n_row * (n_sub - 1)):
            spread(here, k, slot, {"sub": (sub + 1) % n_sub}).wait_send()

    @pl.loop(0, n_block)
    def _(m):
        for t in range(n_col):

            @pl.when(col != t)
            def _():
                s_copy(t, m, True).wait_send()


def per_device(integrals, integral_mask, amplitudes, amplitude_mask, tile_map, row_gap, col_gap, *, n_row, n_sub):
    position = lax.axis_index("col")
    held = amplitudes.shape[0] // TILE
    total = tile_map.shape[0]
    n_col = total // held
    cap = max(1, held // n_col)
    width = col_gap.shape[0]
    rows, depth = integrals.shape
    n_j = n_row * n_sub
    n_block = rows // largest_block(rows, 256)

    every = jnp.arange(total, dtype=jnp.int32)
    owner = tile_map // held
    home = every // held
    earlier = (home[:, None] == home[None, :]) & (owner[:, None] == owner[None, :]) & (every[:, None] < every[None, :])
    rank = jnp.sum(earlier.astype(jnp.int32), axis=0)
    slots = n_col * cap
    line = jnp.arange(2 * slots + held, dtype=jnp.int32)[:, None]
    sent = (home == position)[None, :] & ((owner * cap + rank)[None, :] == line % (slots + held))
    kept = jnp.tile(amplitude_mask.reshape(held), n_col)
    landed = tile_map[None, :] == position * held + line - slots
    index = jnp.sum(
        jnp.where(
            line < slots,
            jnp.where(sent, (every % held)[None, :], 0),
            jnp.where(
                line < slots + held,
                jnp.where(landed, (home * cap + rank)[None, :], 0),
                jnp.where(sent, kept[None, :], 0),
            ),
        ),
        axis=1,
    )

    smem = pl.BlockSpec(memory_space=pltpu.SMEM)
    vmem = pl.BlockSpec(memory_space=pltpu.VMEM)
    dma = pltpu.SemaphoreType.DMA
    return pl.pallas_call(
        functools.partial(kernel, n_col, n_row, n_sub, cap),
        out_shape=jax.ShapeDtypeStruct((rows, width), jnp.bfloat16),
        in_specs=[smem, vmem, vmem, vmem, vmem, pl.BlockSpec(memory_space=pl.ANY)],
        out_specs=vmem,
        scratch_shapes=[
            pltpu.VMEM((rows, depth), jnp.bfloat16),
            pltpu.VMEM((slots, TILE, TILE), jnp.bfloat16),
            pltpu.VMEM((n_j, slots, TILE, TILE), jnp.bfloat16),
            pltpu.VMEM((depth, n_j * TILE), jnp.bfloat16),
            pltpu.VMEM((n_col, rows, width), jnp.bfloat16),
            pltpu.VMEM((2, n_col, rows, width), jnp.bfloat16),
            dma((min(n_col, rows // TILE),)),
            dma((n_col,)),
            dma((n_col,)),
            dma((n_row - 1 + n_row * (n_sub - 1), n_col)),
            dma((n_j, n_col)),
            dma((n_col, n_block)),
            dma((2, n_col, n_block)),
        ],
        compiler_params=pltpu.CompilerParams(
            collective_id=0, has_side_effects=True, vmem_limit_bytes=62 * 1024 * 1024
        ),
        cost_estimate=pl.CostEstimate(
            flops=2 * rows * depth * n_j * TILE, bytes_accessed=2 * rows * depth, transcendentals=0
        ),
    )(
        index,
        integral_mask,
        amplitudes.reshape(held, TILE, TILE),
        row_gap.reshape(rows // TILE, TILE),
        col_gap.reshape(1, width),
        integrals,
    )


def solution(mesh):
    return jax.shard_map(
        functools.partial(per_device, n_row=mesh.shape["row"], n_sub=mesh.shape["sub"]),
        mesh=mesh,
        in_specs=(
            P(("groups", "row", "sub"), "col"),
            P(("groups", "row", "sub"), "col"),
            P(("groups", "col"), ("row", "sub")),
            P(("groups", "col"), ("row", "sub")),
            P(),
            P(("groups", "row", "sub")),
            P(("groups", "col")),
        ),
        out_specs=P(("groups", "row", "sub"), "col"),
        check_vma=False,
    )
```
